512 devices in a mesh: seq: 128 (over z_lo, x, y, core), head: 4 (over z_hi).
Axes of the slice: x: 4, y: 8, z: 8 (z_hi: 4, z_lo: 2; z = z_hi * 2 + z_lo), core: 2. Of those that a mesh axis runs over, the one named last changes fastest.
Arguments:
- queries: bfloat16 [16384, 4096], P('seq', 'head'), may hold values from -6 to 6
- key_rows: bfloat16 [16384, 4096], P('seq', 'head'), may hold values from -6 to 6
- values: bfloat16 [16384, 4096], P('seq', 'head'), may hold values from -11 to 11
- out_grad: bfloat16 [16384, 4096], P('seq', 'head'), may hold values from -11 to 11
- norm_gain: float32 [4096], P('head'), may hold values from 0.1 to 1.9
- head_levels: int32 [32, 7], P('head'), may hold values 0 or 1
Outputs:
- normed: bfloat16 [16384, 4096], P('seq', 'head')
- query_grad: bfloat16 [16384, 4096], P('seq', 'head')
- key_grad: bfloat16 [16384, 4096], P('seq', 'head')
- value_grad: bfloat16 [16384, 4096], P('seq', 'head')
- gain_grad: float32 [4096], P('head')
The draws below stay inside these ranges and needn't reach their ends.
Inputs may be any that keep to these rules, and one draw needn't show every extreme that they name: head_levels[h, l] is 1 where head h reads the block 2**l blocks back.
All inputs are finite; a program needn't handle non-finite values.
Results may differ from the reference program's by a relative error of at most 0.018.
Values may be sent and summed in bfloat16 or wider, within the bound.
A program may use at most 64 MiB of HBM per device.

```python
import math
import jax
import jax.numpy as jnp
from jax import lax

D = 4096
HEADS = 32
HEAD_DIM = 128
TOK_DEV = 128
LEVELS = 7
TOKENS = 16384
N_SEQ = 128


def head_ramp(lowest, ratio):
    head_number = (jnp.arange(D) // HEAD_DIM).astype(jnp.float32)
    return lowest * ratio ** (head_number / (HEADS - 1))


def token_ramp(lowest, ratio):
    position = jnp.arange(TOKENS).astype(jnp.float32)
    return lowest * ratio ** (position / (TOKENS - 1))


def draw_queries(key, part):
    noise_key = jax.random.fold_in(key, 11)
    background = jax.random.truncated_normal(noise_key, -6.0, 6.0, (TOKENS, D), jnp.float32)
    return background.astype(jnp.bfloat16)


def draw_key_rows(key, part):
    noise_key = jax.random.fold_in(key, 12)
    background = jax.random.truncated_normal(noise_key, -6.0, 6.0, (TOKENS, D), jnp.float32)
    return background.astype(jnp.bfloat16)


def draw_values(key, part):
    noise_key = jax.random.fold_in(key, 21)
    background = jax.random.truncated_normal(noise_key, -6.0, 6.0, (TOKENS, D), jnp.float32)
    return (background * head_ramp(0.6, 3.0)[None, :]).astype(jnp.bfloat16)


def draw_out_grad(key, part):
    noise_key = jax.random.fold_in(key, 31)
    background = jax.random.truncated_normal(noise_key, -6.0, 6.0, (TOKENS, D), jnp.float32)
    return (background * token_ramp(0.6, 3.0)[:, None]).astype(jnp.bfloat16)


def set_ends(values, rng, low, largest):
    spot = [jax.random.randint(jax.random.fold_in(rng, axis), (), 0, length) for axis, length in enumerate(values.shape)]
    widest = values.shape.index(max(values.shape))
    beside = spot[:widest] + [(spot[widest] + 1) % values.shape[widest]] + spot[widest + 1:]
    return values.at[tuple(spot)].set(low).at[tuple(beside)].set(largest)


def setup_inputs(seed: int = 0) -> dict:
    seeds = jax.random.split(jax.random.key(seed), 7)
    return {
        "queries": draw_queries(jax.random.fold_in(seeds[6], 71), 0),
        "key_rows": draw_key_rows(jax.random.fold_in(seeds[6], 71), 0),
        "values": draw_values(jax.random.fold_in(seeds[6], 71), 0),
        "out_grad": draw_out_grad(jax.random.fold_in(seeds[6], 71), 0),
        "norm_gain": jnp.clip(1.0 + 0.18 * jax.random.normal(seeds[4], (D,), jnp.float32), 0.1, 1.9),
        "head_levels": set_ends((jax.random.randint(seeds[5], (HEADS, LEVELS), 0, 4) < 3).astype(jnp.int32), jax.random.fold_in(seeds[5], 1), 0, 1),
    }


EPSILON = 1e-06

def stack_near(blocks, block_id, distance):
    source = jnp.maximum(block_id - distance, 0).astype(jnp.int32)
    return jnp.concatenate([blocks[block_id][None], blocks[source]], axis=0)

def near_weights(query_block, near_keys, block_live):
    score_scale = 1.0 / math.sqrt(HEAD_DIM)
    scores = jnp.einsum('qhd,bkhd->hqbk', query_block.astype(jnp.float32), near_keys.astype(jnp.float32)) * score_scale
    row_place = jnp.arange(TOK_DEV, dtype=jnp.int32)
    own_block = (row_place[None, :] <= row_place[:, None])[:, None, :]
    causal = jnp.concatenate([own_block, jnp.ones((TOK_DEV, LEVELS, TOK_DEV), jnp.bool_)], axis=1)
    allowed = block_live.T[:, None, :, None] & causal[None]
    scores = jnp.where(allowed, scores, -jnp.inf)
    row_max = lax.optimization_barrier(jnp.max(scores, axis=(2, 3)))
    raw_weights = jnp.exp(scores - row_max[:, :, None, None])
    row_sum = lax.optimization_barrier(jnp.sum(raw_weights, axis=(2, 3)))
    weights = (raw_weights / row_sum[:, :, None, None]).astype(jnp.bfloat16)
    return (weights, row_max, row_sum)

def reference(queries, key_rows, values, out_grad, norm_gain, head_levels):
    f32 = jnp.float32
    bf16 = jnp.bfloat16
    score_scale = 1.0 / math.sqrt(HEAD_DIM)
    shape_four = (N_SEQ, TOK_DEV, HEADS, HEAD_DIM)
    query_blocks = queries.reshape(shape_four)
    key_blocks = key_rows.reshape(shape_four)
    value_blocks = values.reshape(shape_four)
    distance = 2 ** jnp.arange(LEVELS, dtype=jnp.int32)
    level_on = head_levels.T == 1

    def live_table(block_id):
        valid = block_id - distance >= 0
        return jnp.concatenate([jnp.ones((1, HEADS), jnp.bool_), valid[:, None] & level_on], axis=0)

    def forward_block(block_id):
        near_k = stack_near(key_blocks, block_id, distance)
        near_v = stack_near(value_blocks, block_id, distance)
        weights, row_max, row_sum = near_weights(query_blocks[block_id], near_k, live_table(block_id))
        context = jnp.einsum('hqbk,bkhd->qhd', weights.astype(f32), near_v.astype(f32)).astype(bf16)
        return (context.reshape(TOK_DEV, D), row_max, row_sum)
    block_ids = jnp.arange(N_SEQ, dtype=jnp.int32)
    context_blocks, max_blocks, sum_blocks = lax.map(forward_block, block_ids)
    context = context_blocks.reshape(TOKENS, D)
    context_f = context.astype(f32)
    inverse = lax.rsqrt(lax.optimization_barrier(jnp.sum(context_f * context_f, axis=1)) / D + EPSILON)
    normed = (context_f * inverse[:, None] * norm_gain[None, :]).astype(bf16)
    out_f = out_grad.astype(f32)
    scaled_grad = norm_gain[None, :] * out_f
    correction = lax.optimization_barrier(jnp.sum(scaled_grad * context_f, axis=1))
    context_grad = (inverse[:, None] * scaled_grad - (inverse * inverse * inverse * correction / D)[:, None] * context_f).astype(bf16)
    gain_grad = lax.optimization_barrier(jnp.sum(out_f * context_f * inverse[:, None], axis=0)) / math.sqrt(TOKENS)
    out_dots = lax.optimization_barrier(jnp.sum((context_grad.astype(f32) * context_f).reshape(TOKENS, HEADS, HEAD_DIM), axis=2))
    grad_blocks = context_grad.reshape(shape_four)
    dot_blocks = out_dots.reshape(N_SEQ, TOK_DEV, HEADS)

    def query_side(block_id):
        near_k = stack_near(key_blocks, block_id, distance)
        near_v = stack_near(value_blocks, block_id, distance)
        query_block = query_blocks[block_id]
        weights, row_max, row_sum = near_weights(query_block, near_k, live_table(block_id))
        grad_block = grad_blocks[block_id].astype(f32)
        weight_grad = jnp.einsum('qhd,bkhd->hqbk', grad_block, near_v.astype(f32))
        score_grad = (weights.astype(f32) * (weight_grad - dot_blocks[block_id].T[:, :, None, None]) * score_scale).astype(bf16)
        query_grad = jnp.einsum('hqbk,bkhd->qhd', score_grad.astype(f32), near_k.astype(f32)).astype(bf16)
        key_near = jnp.einsum('hqk,qhd->khd', score_grad[:, :, 0].astype(f32), query_block.astype(f32))
        value_near = jnp.einsum('hqk,qhd->khd', weights[:, :, 0].astype(f32), grad_block)
        return (query_grad.reshape(TOK_DEV, D), key_near, value_near)
    query_grads, key_nears, value_nears = lax.map(query_side, block_ids)

    def key_side(block_id):
        key_block = key_blocks[block_id].astype(f32)
        value_block = value_blocks[block_id].astype(f32)
        key_total = key_nears[block_id]
        value_total = value_nears[block_id]
        for exponent in range(LEVELS):
            source = block_id + 2 ** exponent
            source_ok = source < N_SEQ
            source = jnp.minimum(source, N_SEQ - 1).astype(jnp.int32)
            far_query = query_blocks[source].astype(f32)
            far_grad = grad_blocks[source].astype(f32)
            heads_on = source_ok & level_on[exponent]
            scores = jnp.einsum('qhd,khd->hqk', far_query, key_block) * score_scale
            raw_weights = jnp.exp(scores - max_blocks[source][:, :, None])
            safe_sum = jnp.where(source_ok, sum_blocks[source], 1.0)
            weights = jnp.where(heads_on[:, None, None], raw_weights / safe_sum[:, :, None], 0.0).astype(bf16)
            weight_grad = jnp.einsum('qhd,khd->hqk', far_grad, value_block)
            score_grad = (weights.astype(f32) * (weight_grad - dot_blocks[source].T[:, :, None]) * score_scale).astype(bf16)
            key_part = jnp.einsum('hqk,qhd->khd', score_grad.astype(f32), far_query)
            value_part = jnp.einsum('hqk,qhd->khd', weights.astype(f32), far_grad)
            key_total = key_total + lax.optimization_barrier(key_part.astype(bf16)).astype(f32)
            value_total = value_total + lax.optimization_barrier(value_part.astype(bf16)).astype(f32)
        return (key_total.astype(bf16).reshape(TOK_DEV, D), value_total.astype(bf16).reshape(TOK_DEV, D))
    key_grads, value_grads = lax.map(key_side, block_ids)
    return (normed, query_grads.reshape(TOKENS, D), key_grads.reshape(TOKENS, D), value_grads.reshape(TOKENS, D), gain_grad)
```

```python
import functools
import math

import jax
import jax.numpy as jnp
from jax import lax
from jax.experimental import pallas as pl
from jax.experimental.pallas import tpu as pltpu
from jax.sharding import PartitionSpec as P

D = 4096
HEAD_DIM = 128
EPSILON = 1e-06
MESH = pl.DeviceIdType.MESH
NEG = -1e30
LOG2E = math.log2(math.e)

SLOT = {0: 0, 16: 1, 64: 2, 1: 3, 2: 4, 4: 5, 32: 6, 8: 7}
LEVEL = {1: 0, 2: 1, 4: 2, 8: 3, 16: 4, 32: 5, 64: 6}
STEP_OWN = (0,)
STEPS_FAR = ((16, 64), (1, 2), (4, 32), (8,))
KEYS, VALUES, QUERIES, GRADS, STATS = range(5)
UNROLL = 2


def dot_nt(a, b):
    return lax.dot_general(a, b, (((1,), (1,)), ((), ())), preferred_element_type=jnp.float32)


def dot_nn(a, b):
    return jnp.dot(a, b, preferred_element_type=jnp.float32)


def wide(x, times):
    return x if times == 1 else jnp.concatenate([x] * times, axis=1)


def kernel(
    n_seq,
    n_head,
    heads,
    q_in,
    k_in,
    v_in,
    g_in,
    gain_ref,
    levels_ref,
    normed_ref,
    dq_ref,
    dk_ref,
    dv_ref,
    gain_out,
    kb,
    vb,
    qb,
    gb,
    tb,
    og,
    ctx,
    scores,
    acc,
    mx,
    sm,
    dots,
    dk_acc,
    dv_acc,
    ex,
    gain_acc,
    gain_got,
    send_sem,
    recv_sem,
    local_sem,
    ex_send,
    ex_recv,
    gain_send,
    gain_recv,
):
    f32 = jnp.float32
    bf16 = jnp.bfloat16
    rows = q_in.shape[0]
    dim = HEAD_DIM
    scale = 1.0 / math.sqrt(dim)
    scale2 = scale * LOG2E
    me = lax.axis_index("seq")
    my_head = lax.axis_index("head")
    bufs = {KEYS: kb, VALUES: vb, QUERIES: qb, GRADS: gb, STATS: tb}
    height = {KEYS: rows, VALUES: rows, QUERIES: rows, GRADS: rows, STATS: 2 * heads}
    rounds = len(LEVEL)

    def col(h):
        return pl.ds(pl.multiple_of(h * dim, dim), dim)

    def place(stream):
        return me if stream in (KEYS, VALUES) else n_seq - 1 - me

    def at(stream, spot):
        return spot if stream in (KEYS, VALUES) else n_seq - 1 - spot

    def block(stream, level):
        size = height[stream]
        return bufs[stream].at[pl.ds(SLOT[level] * size, size)]

    def copy(stream, level, source, step):
        target = at(stream, lax.rem(place(stream) + step + n_seq, n_seq))
        return pltpu.make_async_remote_copy(
            src_ref=block(stream, source),
            dst_ref=block(stream, level),
            send_sem=send_sem.at[stream, LEVEL[level]],
            recv_sem=recv_sem.at[stream, LEVEL[level]],
            device_id={"seq": target},
            device_id_type=MESH,
        )

    def edges(stream, level):
        p = place(stream)
        if level == 1:
            even = lax.rem(p, 2) == 0
            return ((0, 1, even), (2, -1, jnp.logical_and(jnp.logical_not(even), p >= 3)))
        source, step = {2: (0, 2), 16: (0, 16), 64: (0, 64), 4: (2, 2), 8: (4, 4), 32: (16, 16)}[level]
        return ((source, step, jnp.logical_and(p >= source, p + step < n_seq)),)

    def send(stream, level, source):
        for origin, step, condition in edges(stream, level):
            if origin == source:
                pl.when(condition)(copy(stream, level, origin, step).start)

    def send_done(stream, level):
        for origin, step, condition in edges(stream, level):
            pl.when(condition)(copy(stream, level, origin, step).wait_send)

    def got(stream, level):
        pl.when(place(stream) >= level)(copy(stream, level, 0, 2).wait_recv)

    loads = [
        pltpu.make_async_copy(k_in, block(KEYS, 0), local_sem.at[0]),
        pltpu.make_async_copy(v_in, block(VALUES, 0), local_sem.at[1]),
        pltpu.make_async_copy(q_in, block(QUERIES, 0), local_sem.at[2]),
        pltpu.make_async_copy(g_in, og, local_sem.at[3]),
    ]
    for load in loads:
        load.start()

    def swap(bit):
        return me + bit - 2 * bit * lax.rem(me // bit, 2)

    barrier = pltpu.get_barrier_semaphore()
    greeted = 0
    for step in (2, n_seq - 2, 4, n_seq - 4, 16, n_seq - 16, 64):
        pl.semaphore_signal(
            barrier, inc=1, device_id={"seq": lax.rem(me + step, n_seq)}, device_id_type=MESH
        )
        greeted += 1
    for bit in (1, 2, 4, 8, 16, 32):
        pl.semaphore_signal(barrier, inc=1, device_id={"seq": swap(bit)}, device_id_type=MESH)
        greeted += 1
    for step in range(1, n_head):
        pl.semaphore_signal(
            barrier, inc=1, device_id={"head": lax.rem(my_head + step, n_head)}, device_id_type=MESH
        )
        greeted += 1

    for stream in (KEYS, VALUES, QUERIES, GRADS, STATS):
        for level in LEVEL:

            @pl.when(place(stream) < level)
            def _(stream=stream, level=level):
                ref = block(stream, level)
                ref[...] = jnp.zeros(ref.shape, ref.dtype)

    for load in loads:
        load.wait()
    pl.semaphore_wait(barrier, greeted)

    for level in (2, 1, 16, 64):
        send(KEYS, level, 0)
        send(VALUES, level, 0)
    for level in (2, 1, 16, 64):
        send(QUERIES, level, 0)

    def bias_of(h, level, stream):
        if level == 0:
            return jnp.float32(0.0)
        live = jnp.logical_and(levels_ref[h, LEVEL[level]] == 1, place(stream) >= level)
        return jnp.where(live, jnp.float32(0.0), jnp.float32(NEG))

    row_id = lax.broadcasted_iota(jnp.int32, (rows, rows), 0)
    col_id = lax.broadcasted_iota(jnp.int32, (rows, rows), 1)

    def each_head(body):
        def some(i, carry):
            for j in range(UNROLL):
                body(i * UNROLL + j)
            return carry

        lax.fori_loop(0, heads // UNROLL, some, 0)

    def forward_step(step):
        first = step == STEP_OWN
        top = SLOT[step[0]] * rows
        count = len(step) * rows

        def one(h):
            q = qb[0:rows, col(h)]
            k = kb[top : top + count, col(h)]
            v = vb[top : top + count, col(h)]
            s = dot_nt(q, k) * scale2
            if first:
                s = jnp.where(col_id <= row_id, s, NEG)
                high = s
            else:
                parts = [
                    s[:, j * rows : (j + 1) * rows] + bias_of(h, level, KEYS)
                    for j, level in enumerate(step)
                ]
                high = functools.reduce(jnp.maximum, parts)
                s = parts[0] if len(parts) == 1 else jnp.concatenate(parts, axis=1)
            scores[h, :, top : top + count] = s
            new = jnp.broadcast_to(jnp.max(high, axis=1, keepdims=True), (rows, dim))
            if not first:
                old = mx[h]
                new = jnp.maximum(old, new)
            p = jnp.exp2(s - wide(new, len(step)))
            total = functools.reduce(
                jnp.add, [p[:, j * rows : (j + 1) * rows] for j in range(len(step))]
            )
            total = jnp.broadcast_to(jnp.sum(total, axis=1, keepdims=True), (rows, dim))
            out = dot_nn(p.astype(bf16), v)
            if first:
                acc[:, col(h)] = out
                sm[h] = total
            else:
                fade = jnp.exp2(old - new)
                acc[:, col(h)] = acc[:, col(h)] * fade + out
                sm[h] = sm[h] * fade + total
            mx[h] = new

        each_head(one)

    forward_step(STEP_OWN)
    for stream in (KEYS, VALUES):
        got(stream, 2)
        send(stream, 4, 2)
        send(stream, 1, 2)
    for stream in (KEYS, VALUES):
        got(stream, 16)
        send(stream, 32, 16)
    got(QUERIES, 2)
    send(QUERIES, 4, 2)
    send(QUERIES, 1, 2)
    got(QUERIES, 16)
    send(QUERIES, 32, 16)
    for stream in (KEYS, VALUES):
        got(stream, 64)
    forward_step((16, 64))
    got(QUERIES, 4)
    send(QUERIES, 8, 4)
    got(KEYS, 1)
    got(VALUES, 1)
    forward_step((1, 2))
    for stream in (KEYS, VALUES):
        got(stream, 4)
        send(stream, 8, 4)
    got(KEYS, 32)
    got(VALUES, 32)
    forward_step((4, 32))
    got(KEYS, 8)
    got(VALUES, 8)
    forward_step((8,))

    def finish(h, carry):
        squares, pulls = carry
        total = sm[h]
        c = (acc[:, col(h)] * (1.0 / total)).astype(bf16)
        ctx[:, col(h)] = c
        c = c.astype(f32)
        lse = mx[h] + jnp.log2(total)
        mx[h] = lse
        tb[pl.ds(h, 1), :] = lse.T[0:1, :]
        pull = gain_ref[0:1, col(h)] * og[:, col(h)].astype(f32) * c
        return squares + c * c, pulls + pull

    zero = jnp.zeros((rows, dim), f32)
    squares, pulls = lax.fori_loop(0, heads, finish, (zero, zero))
    ex[0, 0:1, :] = jnp.sum(squares.T, axis=0, keepdims=True)
    ex[0, 1:2, :] = jnp.sum(pulls.T, axis=0, keepdims=True)
    ex[0, 2:8, :] = jnp.zeros((6, rows), f32)
    swaps = [
        pltpu.make_async_remote_copy(
            src_ref=ex.at[0],
            dst_ref=ex.at[step],
            send_sem=ex_send.at[step],
            recv_sem=ex_recv.at[step],
            device_id={"head": lax.rem(my_head + step, n_head)},
            device_id_type=MESH,
        )
        for step in range(1, n_head)
    ]
    for one in swaps:
        one.start()
    for one in swaps:
        one.wait()
    whole = functools.reduce(jnp.add, [ex[step] for step in range(n_head)])
    inverse_row = lax.rsqrt(whole[0:1, :] / D + EPSILON)
    pull_row = inverse_row * inverse_row * inverse_row * whole[1:2, :] / D
    inverse = jnp.broadcast_to(inverse_row, (dim, rows)).T
    pull_back = jnp.broadcast_to(pull_row, (dim, rows)).T

    def make_grad(h):
        c = ctx[:, col(h)].astype(f32)
        scaled = gain_ref[0:1, col(h)] * og[:, col(h)].astype(f32)
        gb[0:rows, col(h)] = (inverse * scaled - pull_back * c).astype(bf16)

    each_head(make_grad)
    for level in (2, 1, 16, 64):
        send(GRADS, level, 0)

    def make_dots(h):
        c = ctx[:, col(h)].astype(f32)
        both = gb[0:rows, col(h)].astype(f32) * c
        row = jnp.sum(both.T, axis=0, keepdims=True)
        tb[pl.ds(heads + h, 1), :] = row
        dots[h] = jnp.broadcast_to(row, (dim, rows)).T

    each_head(make_dots)
    for level in (2, 1, 16, 64):
        send(STATS, level, 0)

    def make_normed(h):
        c = ctx[:, col(h)].astype(f32) * inverse
        normed_ref[:, col(h)] = (c * gain_ref[0:1, col(h)]).astype(bf16)
        gain_acc[0, 0:1, col(h)] = jnp.sum(og[:, col(h)].astype(f32) * c, axis=0, keepdims=True)

    each_head(make_normed)

    def gain_copy(r):
        return pltpu.make_async_remote_copy(
            src_ref=gain_acc.at[r],
            dst_ref=gain_got.at[r],
            send_sem=gain_send.at[r],
            recv_sem=gain_recv.at[r],
            device_id={"seq": swap(2**r)},
            device_id_type=MESH,
        )

    def gain_next(r):
        gain_copy(r).wait()
        gain_acc[r + 1] = gain_acc[r] + gain_got[r]
        if r + 1 < rounds:
            gain_copy(r + 1).start()

    gain_copy(0).start()

    def query_side(h):
        g = gb[0:rows, col(h)]
        lse = mx[h]
        dot = dots[h]
        total = jnp.zeros((rows, dim), f32)
        for j in range(0, len(SLOT), 2):
            span = slice(j * rows, (j + 2) * rows)
            pull = dot_nt(g, vb[span, col(h)])
            p = jnp.exp2(scores[h, :, span] - wide(lse, 2))
            ds = (p * (pull - wide(dot, 2))).astype(bf16)
            total = total + dot_nn(ds, kb[span, col(h)])
        dq_ref[:, col(h)] = (total * scale).astype(bf16)

    def key_step(step):
        first = step == STEP_OWN
        slot = SLOT[step[0]]
        top = slot * rows
        count = len(step) * rows

        def one(h):
            k = kb[0:rows, col(h)]
            v = vb[0:rows, col(h)]
            q = qb[top : top + count, col(h)]
            g = gb[top : top + count, col(h)]
            shift = []
            dot = []
            for j, level in enumerate(step):
                base = (slot + j) * 2 * heads
                shift.append(bias_of(h, level, QUERIES) - tb[pl.ds(base + h, 1), :])
                dot.append(tb[pl.ds(base + heads + h, 1), :])
            shift = wide(shift[0], 1) if len(step) == 1 else jnp.concatenate(shift, axis=1)
            dot = wide(dot[0], 1) if len(step) == 1 else jnp.concatenate(dot, axis=1)
            s = dot_nt(k, q) * scale2 + shift
            if first:
                s = jnp.where(row_id <= col_id, s, NEG)
            p = jnp.exp2(s)
            pull = dot_nt(v, g)
            ds = (p * (pull - dot)).astype(bf16)
            dv = dot_nn(p.astype(bf16), g)
            dk = dot_nn(ds, q)
            if first:
                dv_acc[:, col(h)] = dv
                dk_acc[:, col(h)] = dk
            elif step == STEPS_FAR[-1]:
                dv_ref[:, col(h)] = (dv_acc[:, col(h)] + dv).astype(bf16)
                dk_ref[:, col(h)] = ((dk_acc[:, col(h)] + dk) * scale).astype(bf16)
            else:
                dv_acc[:, col(h)] += dv
                dk_acc[:, col(h)] += dk

        each_head(one)

    key_step(STEP_OWN)
    gain_next(0)
    for stream in (GRADS, STATS):
        got(stream, 2)
        send(stream, 4, 2)
        send(stream, 1, 2)
    for stream in (GRADS, STATS):
        got(stream, 16)
        send(stream, 32, 16)
    gain_next(1)
    each_head(query_side)
    gain_next(2)
    for stream in (GRADS, STATS):
        got(stream, 4)
        send(stream, 8, 4)
    gain_next(3)
    for stream in (QUERIES, GRADS, STATS):
        got(stream, 64)
    key_step((16, 64))
    gain_next(4)
    for stream in (QUERIES, GRADS, STATS):
        got(stream, 1)
    key_step((1, 2))
    gain_next(5)
    for stream in (QUERIES, GRADS, STATS):
        got(stream, 32)
    key_step((4, 32))
    gain_next(6)
    gain_out[...] = gain_acc[rounds] * (1.0 / math.sqrt(n_seq * rows))
    for stream in (QUERIES, GRADS, STATS):
        got(stream, 8)
    key_step((8,))

    for stream in (KEYS, VALUES, QUERIES, GRADS, STATS):
        for level in LEVEL:
            send_done(stream, level)


def body(queries, key_rows, values, out_grad, norm_gain, head_levels):
    f32 = jnp.float32
    bf16 = jnp.bfloat16
    rows, width = queries.shape
    heads = width // HEAD_DIM
    n_seq = lax.axis_size("seq")
    n_head = lax.axis_size("head")
    slots = len(SLOT)
    rounds = len(LEVEL)
    full = jax.ShapeDtypeStruct((rows, width), bf16)
    anywhere = pl.BlockSpec(memory_space=pl.ANY)
    vmem = pl.BlockSpec(memory_space=pltpu.VMEM)
    smem = pl.BlockSpec(memory_space=pltpu.SMEM)
    normed, dq, dk, dv, gain = pl.pallas_call(
        functools.partial(kernel, n_seq, n_head, heads),
        out_shape=(full, full, full, full, jax.ShapeDtypeStruct((1, width), f32)),
        in_specs=[anywhere] * 4 + [vmem, smem],
        out_specs=[vmem] * 5,
        scratch_shapes=[
            pltpu.VMEM((slots * rows, width), bf16),
            pltpu.VMEM((slots * rows, width), bf16),
            pltpu.VMEM((slots * rows, width), bf16),
            pltpu.VMEM((slots * rows, width), bf16),
            pltpu.VMEM((slots * 2 * heads, rows), f32),
            pltpu.VMEM((rows, width), bf16),
            pltpu.VMEM((rows, width), bf16),
            pltpu.VMEM((heads, rows, slots * rows), f32),
            pltpu.VMEM((rows, width), f32),
            pltpu.VMEM((heads, rows, HEAD_DIM), f32),
            pltpu.VMEM((heads, rows, HEAD_DIM), f32),
            pltpu.VMEM((heads, rows, HEAD_DIM), f32),
            pltpu.VMEM((rows, width), f32),
            pltpu.VMEM((rows, width), f32),
            pltpu.VMEM((n_head, 8, rows), f32),
            pltpu.VMEM((rounds + 1, 1, width), f32),
            pltpu.VMEM((rounds, 1, width), f32),
            pltpu.SemaphoreType.DMA((5, rounds)),
            pltpu.SemaphoreType.DMA((5, rounds)),
            pltpu.SemaphoreType.DMA((4,)),
            pltpu.SemaphoreType.DMA((n_head,)),
            pltpu.SemaphoreType.DMA((n_head,)),
            pltpu.SemaphoreType.DMA((rounds,)),
            pltpu.SemaphoreType.DMA((rounds,)),
        ],
        compiler_params=pltpu.CompilerParams(
            collective_id=0, has_side_effects=True, vmem_limit_bytes=48 * 2**20
        ),
        name="logsparse_layer",
    )(queries, key_rows, values, out_grad, norm_gain.reshape(1, width), head_levels)
    return normed, dq, dk, dv, gain.reshape(width)


def solution(mesh):
    placed = (
        P("seq", "head"),
        P("seq", "head"),
        P("seq", "head"),
        P("seq", "head"),
        P("head"),
        P("head", None),
    )
    return jax.shard_map(
        body,
        mesh=mesh,
        in_specs=placed,
        out_specs=(
            P("seq", "head"),
            P("seq", "head"),
            P("seq", "head"),
            P("seq", "head"),
            P("head"),
        ),
        check_vma=False,
    )
```

```python
import functools
import math

import jax
import jax.numpy as jnp
from jax import lax
from jax.experimental import pallas as pl
from jax.experimental.pallas import tpu as pltpu
from jax.sharding import PartitionSpec as P

D = 4096
HEAD_DIM = 128
EPSILON = 1e-06
MESH = pl.DeviceIdType.MESH
NEG = -1e30
LOG2E = math.log2(math.e)

VIA8, VIA32 = "via8", "via32"
SLOT = {0: 0, 16: 1, 64: 2, 1: 3, 2: 4, 4: 5, 32: 6, 8: 7, VIA8: 8, VIA32: 9}
BLOCKS = 8
LEVEL = {1: 0, 2: 1, 4: 2, 8: 3, 16: 4, 32: 5, 64: 6}
SEM = {**LEVEL, VIA8: 7, VIA32: 8}
RING = 16
STEP_OWN = (0,)
STEPS_FAR = ((16, 64), (1, 2), (4, 32), (8,))
KEYS, VALUES, QUERIES, GRADS, STATS = range(5)
CHUNKS = 4
AROUND = (2, 3)
FORWARD = tuple((array, chunk) for chunk in range(CHUNKS) for array in (KEYS, VALUES))
BACKWARD = tuple((GRADS, chunk) for chunk in range(CHUNKS))
DIRECT = ((QUERIES, 0), (STATS, 0))
STREAMS = FORWARD + BACKWARD + DIRECT
SEMS = {stream: i for i, stream in enumerate(STREAMS)}


def dot_nt(a, b):
    return lax.dot_general(a, b, (((1,), (1,)), ((), ())), preferred_element_type=jnp.float32)


def dot_nn(a, b):
    return jnp.dot(a, b, preferred_element_type=jnp.float32)


def wide(x, times):
    return x if times == 1 else jnp.concatenate([x] * times, axis=1)


def kernel(
    n_seq,
    n_head,
    heads,
    q_in,
    k_in,
    v_in,
    g_in,
    gain_in,
    levels_in,
    normed_ref,
    dq_ref,
    dk_ref,
    dv_ref,
    gain_out,
    kb,
    vb,
    qb,
    gb,
    tb,
    og,
    gain_ref,
    levels_ref,
    ctx,
    scores,
    acc,
    mx,
    sm,
    dots,
    dk_acc,
    dv_acc,
    ex,
    gain_acc,
    gain_got,
    send_sem,
    recv_sem,
    local_sem,
    ex_send,
    ex_recv,
    gain_send,
    gain_recv,
):
    f32 = jnp.float32
    bf16 = jnp.bfloat16
    rows = q_in.shape[0]
    dim = HEAD_DIM
    scale = 1.0 / math.sqrt(dim)
    scale2 = scale * LOG2E
    me = lax.axis_index("seq")
    my_head = lax.axis_index("head")
    part = heads * dim // CHUNKS
    bufs = {KEYS: kb, VALUES: vb, QUERIES: qb, GRADS: gb, STATS: tb}

    def col(h):
        return pl.ds(pl.multiple_of(h * dim, dim), dim)

    def place(stream):
        return me if stream[0] in (KEYS, VALUES) else n_seq - 1 - me

    def at(stream, spot):
        return spot if stream[0] in (KEYS, VALUES) else n_seq - 1 - spot

    def block(stream, level):
        array, chunk = stream
        size = 2 * heads if array == STATS else rows
        span = pl.ds(SLOT[level] * size, size)
        if stream in DIRECT:
            return bufs[array].at[span] if array == STATS else bufs[array].at[:, span]
        return bufs[array].at[chunk, span]

    def copy(stream, level, source, target):
        return pltpu.make_async_remote_copy(
            src_ref=block(stream, source),
            dst_ref=block(stream, level),
            send_sem=send_sem.at[SEMS[stream], SEM[level]],
            recv_sem=recv_sem.at[SEMS[stream], SEM[level]],
            device_id={"seq": at(stream, target)},
            device_id_type=MESH,
        )

    def spot(stream):
        p = place(stream)
        y = lax.rem(p // 2, 8)
        return p, y, lax.rem(p // RING, 4), p - lax.rem(p, RING)

    def in_ring(p, by):
        y = lax.rem(p // 2 + by, 8)
        return p - lax.rem(p, RING) + 2 * y + lax.rem(p, 2)

    def edges(stream, level):
        p, y, x, base = spot(stream)
        if stream in DIRECT:
            return ((0, p + level, p + level < n_seq),) if level in LEVEL else ()
        if level == 1:
            even = lax.rem(p, 2) == 0
            return ((0, p + 1, even), (2, p - 1, jnp.logical_and(jnp.logical_not(even), p >= 3)))
        if level == 2:
            last = y == 7
            return (
                (0, p + 2, jnp.logical_not(last)),
                (16, p - 14, jnp.logical_and(last, p >= 16)),
            )
        if stream[1] in AROUND:
            if level == VIA8:
                low = y < 4
                target = in_ring(p, 7)
                return (
                    (0, target, low),
                    (16, target, jnp.logical_and(jnp.logical_not(low), base >= RING)),
                )
            if level == 8:
                return ((VIA8, in_ring(p, 5), arrives(stream, VIA8)),)
            if level == VIA32:
                return ((0, jnp.where(x == 0, p + 48, p - 16), p + 32 < n_seq),)
            if level == 32:
                return ((VIA32, jnp.where(x == 3, p - 16, p + 48), arrives(stream, VIA32)),)
        elif level in (VIA8, VIA32):
            return ()
        source, step = {16: (0, 16), 64: (0, 64), 4: (2, 2), 8: (4, 4), 32: (16, 16)}[level]
        return ((source, p + step, jnp.logical_and(p >= source, p + step < n_seq)),)

    def arrives(stream, level):
        p, y, x, base = spot(stream)
        if level == VIA8:
            return jnp.logical_or(jnp.logical_or(y <= 2, y == 7), base >= RING)
        if level == VIA32:
            return jnp.where(x == 3, p - 48, p + 16) + 32 < n_seq
        return p >= level

    def send(stream, level, source):
        for origin, target, condition in edges(stream, level):
            if origin == source:
                pl.when(condition)(copy(stream, level, origin, target).start)

    def send_done(stream, level):
        for origin, target, condition in edges(stream, level):
            pl.when(condition)(copy(stream, level, origin, target).wait_send)

    def got(stream, level):
        if level in LEVEL or (stream not in DIRECT and stream[1] in AROUND):
            there = in_ring(place(stream), 1)
            pl.when(arrives(stream, level))(copy(stream, level, 0, there).wait_recv)

    def pass_on(stream, level):
        got(stream, level)
        for onward in SEM:
            send(stream, onward, level)

    loads = [
        pltpu.make_async_copy(source, target, local_sem.at[i])
        for i, (source, target) in enumerate(
            (
                *(
                    (source.at[:, pl.ds(i * part, part)], target.at[i, pl.ds(0, rows)])
                    for source, target in ((k_in, kb), (v_in, vb), (q_in, qb))
                    for i in range(CHUNKS)
                ),
                (g_in, og),
                (gain_in, gain_ref),
                (levels_in, levels_ref),
            )
        )
    ]
    for load in loads:
        load.start()

    my_core, my_y, my_x, my_z = lax.rem(me, 2), lax.rem(me // 2, 8), lax.rem(me // RING, 4), me // (4 * RING)
    groups = (
        (8, my_y, lambda i: me - 2 * my_y + 2 * i),
        (4, 2 * my_z + my_core, lambda i: me + 4 * RING * (i // 2 - my_z) + lax.rem(i, 2) - my_core),
        (4, my_x, lambda i: me + RING * (i - my_x)),
    )

    barrier = pltpu.get_barrier_semaphore()
    greeted = 0
    partners = [lax.rem(me + step, n_seq) for step in (1, 2, 4, 8, 16, 32, 48)]
    partners += [lax.rem(me + n_seq - step, n_seq) for step in (1, 2, 4, 8, 16, 32, 48, 64)]
    partners.append(me + 1 - 2 * my_core)
    partners += [in_ring(me, by) for by in (1, 3, 5, 7)]
    for size, mine, member in groups:
        partners += [member(lax.rem(mine + i, size)) for i in range(1, size)]
    for partner in partners:
        pl.semaphore_signal(barrier, inc=1, device_id={"seq": partner}, device_id_type=MESH)
        greeted += 1
    for step in range(1, n_head):
        pl.semaphore_signal(
            barrier, inc=1, device_id={"head": lax.rem(my_head + step, n_head)}, device_id_type=MESH
        )
        greeted += 1

    for array in bufs:
        size = 2 * heads if array == STATS else rows
        for level in LEVEL:

            @pl.when(place((array, 0)) < level)
            def _(ref=bufs[array], span=pl.ds(SLOT[level] * size, size)):
                if array == STATS:
                    ref[span, :] = jnp.zeros((size, ref.shape[1]), ref.dtype)
                else:
                    for i in range(CHUNKS):
                        ref[i, span, :] = jnp.zeros((size, part), ref.dtype)

    for load in loads:
        load.wait()
    pl.semaphore_wait(barrier, greeted)

    own_order = (16, 64, 2, VIA8, VIA32, 1)
    for level in own_order:
        for stream in FORWARD:
            send(stream, level, 0)

    def bias_of(h, level, stream):
        if level == 0:
            return jnp.float32(0.0)
        live = jnp.logical_and(levels_ref[h, LEVEL[level]] == 1, place(stream) >= level)
        return jnp.where(live, jnp.float32(0.0), jnp.float32(NEG))

    row_id = lax.broadcasted_iota(jnp.int32, (rows, rows), 0)
    col_id = lax.broadcasted_iota(jnp.int32, (rows, rows), 1)

    per_chunk = heads // CHUNKS

    def each_head(body):
        def some(i, carry):
            for j in range(per_chunk):
                body(i * per_chunk + j, lambda ref, span: ref[i, span, j * dim : (j + 1) * dim])
            return carry

        lax.fori_loop(0, CHUNKS, some, 0)

    def forward_step(step):
        first = step == STEP_OWN
        top = SLOT[step[0]] * rows
        count = len(step) * rows

        def one(h, of):
            q = of(qb, slice(0, rows))
            k = of(kb, slice(top, top + count))
            v = of(vb, slice(top, top + count))
            s = dot_nt(q, k) * scale2
            if first:
                s = jnp.where(col_id <= row_id, s, NEG)
                high = s
            else:
                parts = [
                    s[:, j * rows : (j + 1) * rows] + bias_of(h, level, (KEYS, 0))
                    for j, level in enumerate(step)
                ]
                high = functools.reduce(jnp.maximum, parts)
                s = parts[0] if len(parts) == 1 else jnp.concatenate(parts, axis=1)
            scores[h, :, top : top + count] = s
            new = jnp.broadcast_to(jnp.max(high, axis=1, keepdims=True), (rows, dim))
            if not first:
                old = mx[h]
                new = jnp.maximum(old, new)
            p = jnp.exp2(s - wide(new, len(step)))
            total = functools.reduce(
                jnp.add, [p[:, j * rows : (j + 1) * rows] for j in range(len(step))]
            )
            total = jnp.broadcast_to(jnp.sum(total, axis=1, keepdims=True), (rows, dim))
            out = dot_nn(p.astype(bf16), v)
            if first:
                acc[:, col(h)] = out
                sm[h] = total
            else:
                fade = jnp.exp2(old - new)
                acc[:, col(h)] = acc[:, col(h)] * fade + out
                sm[h] = sm[h] * fade + total
            mx[h] = new

        each_head(one)

    forward_step(STEP_OWN)
    for stream in FORWARD:
        for level in (16, 2, VIA8, VIA32):
            pass_on(stream, level)
    for stream in FORWARD:
        got(stream, 64)
    forward_step((16, 64))
    for stream in FORWARD:
        pass_on(stream, 4)
    for level in (8, 4, 2, 1, 32, 16, 64):
        send((QUERIES, 0), level, 0)
    for stream in FORWARD:
        got(stream, 1)
    forward_step((1, 2))
    for stream in FORWARD:
        got(stream, 32)
    forward_step((4, 32))
    for stream in FORWARD:
        got(stream, 8)
    forward_step((8,))

    def finish(h, carry):
        squares, pulls = carry
        total = sm[h]
        c = (acc[:, col(h)] * (1.0 / total)).astype(bf16)
        ctx[:, col(h)] = c
        c = c.astype(f32)
        lse = mx[h] + jnp.log2(total)
        mx[h] = lse
        tb[pl.ds(h, 1), :] = lse.T[0:1, :]
        pull = gain_ref[0:1, col(h)] * og[:, col(h)].astype(f32) * c
        return squares + c * c, pulls + pull

    zero = jnp.zeros((rows, dim), f32)
    squares, pulls = lax.fori_loop(0, heads, finish, (zero, zero))
    ex[0, 0:1, :] = jnp.sum(squares.T, axis=0, keepdims=True)
    ex[0, 1:2, :] = jnp.sum(pulls.T, axis=0, keepdims=True)
    ex[0, 2:8, :] = jnp.zeros((6, rows), f32)
    swaps = [
        pltpu.make_async_remote_copy(
            src_ref=ex.at[0],
            dst_ref=ex.at[step],
            send_sem=ex_send.at[step],
            recv_sem=ex_recv.at[step],
            device_id={"head": lax.rem(my_head + step, n_head)},
            device_id_type=MESH,
        )
        for step in range(1, n_head)
    ]
    for one in swaps:
        one.start()
    for one in swaps:
        one.wait()
    whole = functools.reduce(jnp.add, [ex[step] for step in range(n_head)])
    inverse_row = lax.rsqrt(whole[0:1, :] / D + EPSILON)
    pull_row = inverse_row * inverse_row * inverse_row * whole[1:2, :] / D
    inverse = jnp.broadcast_to(inverse_row, (dim, rows)).T
    pull_back = jnp.broadcast_to(pull_row, (dim, rows)).T

    def make_grad(chunk, j):
        h = chunk * per_chunk + j
        c = ctx[:, col(h)].astype(f32)
        scaled = gain_ref[0:1, col(h)] * og[:, col(h)].astype(f32)
        gb[chunk, 0:rows, j * dim : (j + 1) * dim] = (inverse * scaled - pull_back * c).astype(bf16)

    for stream in BACKWARD:
        for i in range(per_chunk):
            make_grad(stream[1], i)
        for level in own_order:
            send(stream, level, 0)

    def make_dots(h, of):
        c = ctx[:, col(h)].astype(f32)
        both = of(gb, slice(0, rows)).astype(f32) * c
        row = jnp.sum(both.T, axis=0, keepdims=True)
        tb[pl.ds(heads + h, 1), :] = row
        dots[h] = jnp.broadcast_to(row, (dim, rows)).T

    each_head(make_dots)
    for level in (8, 4, 2, 1, 32, 16, 64):
        send((STATS, 0), level, 0)

    def make_normed(h, of):
        c = ctx[:, col(h)].astype(f32) * inverse
        normed_ref[:, col(h)] = (c * gain_ref[0:1, col(h)]).astype(bf16)
        gain_acc[0:1, col(h)] = jnp.sum(og[:, col(h)].astype(f32) * c, axis=0, keepdims=True)

    each_head(make_normed)

    def gain_copies(r):
        size, mine, member = groups[r]
        first = sum(group[0] for group in groups[:r])
        return first, [
            pltpu.make_async_remote_copy(
                src_ref=gain_acc,
                dst_ref=gain_got.at[first + mine],
                send_sem=gain_send.at[first + i],
                recv_sem=gain_recv.at[first + i],
                device_id={"seq": member(lax.rem(mine + i, size))},
                device_id_type=MESH,
            )
            for i in range(1, size)
        ]

    def gain_start(r):
        first, copies = gain_copies(r)
        for one in copies:
            one.start()
        gain_got[first + groups[r][1]] = gain_acc[...]

    def gain_end(r):
        first, copies = gain_copies(r)
        for one in copies:
            one.wait()
        gain_acc[...] = functools.reduce(
            jnp.add, [gain_got[first + i] for i in range(groups[r][0])]
        )

    gain_start(0)

    def query_side(h, of):
        g = of(gb, slice(0, rows))
        lse = mx[h]
        dot = dots[h]
        total = jnp.zeros((rows, dim), f32)
        for j in range(0, BLOCKS, 2):
            span = slice(j * rows, (j + 2) * rows)
            pull = dot_nt(g, of(vb, span))
            p = jnp.exp2(scores[h, :, span] - wide(lse, 2))
            ds = (p * (pull - wide(dot, 2))).astype(bf16)
            total = total + dot_nn(ds, of(kb, span))
        dq_ref[:, col(h)] = (total * scale).astype(bf16)

    def key_step(step):
        first = step == STEP_OWN
        slot = SLOT[step[0]]
        top = slot * rows
        count = len(step) * rows

        def one(h, of):
            k = of(kb, slice(0, rows))
            v = of(vb, slice(0, rows))
            q = of(qb, slice(top, top + count))
            g = of(gb, slice(top, top + count))
            shift = []
            dot = []
            for j, level in enumerate(step):
                base = (slot + j) * 2 * heads
                shift.append(bias_of(h, level, (QUERIES, 0)) - tb[pl.ds(base + h, 1), :])
                dot.append(tb[pl.ds(base + heads + h, 1), :])
            shift = wide(shift[0], 1) if len(step) == 1 else jnp.concatenate(shift, axis=1)
            dot = wide(dot[0], 1) if len(step) == 1 else jnp.concatenate(dot, axis=1)
            s = dot_nt(k, q) * scale2 + shift
            if first:
                s = jnp.where(row_id <= col_id, s, NEG)
            p = jnp.exp2(s)
            pull = dot_nt(v, g)
            ds = (p * (pull - dot)).astype(bf16)
            dv = dot_nn(p.astype(bf16), g)
            dk = dot_nn(ds, q)
            if first:
                dv_acc[:, col(h)] = dv
                dk_acc[:, col(h)] = dk
            elif step == STEPS_FAR[-1]:
                dv_ref[:, col(h)] = (dv_acc[:, col(h)] + dv).astype(bf16)
                dk_ref[:, col(h)] = ((dk_acc[:, col(h)] + dk) * scale).astype(bf16)
            else:
                dv_acc[:, col(h)] += dv
                dk_acc[:, col(h)] += dk

        each_head(one)

    def key_got(level):
        for stream in BACKWARD + DIRECT:
            got(stream, level)

    for stream in BACKWARD:
        for level in (16, 2, VIA8, VIA32):
            pass_on(stream, level)
    key_step(STEP_OWN)
    gain_end(0)
    gain_start(1)
    for stream in BACKWARD:
        pass_on(stream, 4)
    each_head(query_side)
    gain_end(1)
    gain_start(2)
    for stream in DIRECT:
        for level in (16, 2, 4):
            got(stream, level)
    key_got(64)
    key_step((16, 64))
    key_got(1)
    key_step((1, 2))
    gain_end(2)
    gain_out[...] = gain_acc[...] * (1.0 / math.sqrt(n_seq * rows))
    key_got(32)
    key_step((4, 32))
    key_got(8)
    key_step((8,))

    for stream in STREAMS:
        for level in SEM:
            send_done(stream, level)


def body(queries, key_rows, values, out_grad, norm_gain, head_levels):
    f32 = jnp.float32
    bf16 = jnp.bfloat16
    rows, width = queries.shape
    heads = width // HEAD_DIM
    n_seq = lax.axis_size("seq")
    n_head = lax.axis_size("head")
    slots = BLOCKS
    stops = len(SLOT)
    full = jax.ShapeDtypeStruct((rows, width), bf16)
    hbm = pl.BlockSpec(memory_space=pltpu.HBM)
    vmem = pl.BlockSpec(memory_space=pltpu.VMEM)
    normed, dq, dk, dv, gain = pl.pallas_call(
        functools.partial(kernel, n_seq, n_head, heads),
        out_shape=(full, full, full, full, jax.ShapeDtypeStruct((1, width), f32)),
        in_specs=[hbm] * 6,
        out_specs=[vmem] * 5,
        scratch_shapes=[
            pltpu.VMEM((CHUNKS, stops * rows, width // CHUNKS), bf16),
            pltpu.VMEM((CHUNKS, stops * rows, width // CHUNKS), bf16),
            pltpu.VMEM((CHUNKS, slots * rows, width // CHUNKS), bf16),
            pltpu.VMEM((CHUNKS, stops * rows, width // CHUNKS), bf16),
            pltpu.VMEM((slots * 2 * heads, rows), f32),
            pltpu.VMEM((rows, width), bf16),
            pltpu.VMEM((1, width), f32),
            pltpu.SMEM(head_levels.shape, jnp.int32),
            pltpu.VMEM((rows, width), bf16),
            pltpu.VMEM((heads, rows, slots * rows), f32),
            pltpu.VMEM((rows, width), f32),
            pltpu.VMEM((heads, rows, HEAD_DIM), f32),
            pltpu.VMEM((heads, rows, HEAD_DIM), f32),
            pltpu.VMEM((heads, rows, HEAD_DIM), f32),
            pltpu.VMEM((rows, width), f32),
            pltpu.VMEM((rows, width), f32),
            pltpu.VMEM((n_head, 8, rows), f32),
            pltpu.VMEM((1, width), f32),
            pltpu.VMEM((16, 1, width), f32),
            pltpu.SemaphoreType.DMA((len(STREAMS), len(SEM))),
            pltpu.SemaphoreType.DMA((len(STREAMS), len(SEM))),
            pltpu.SemaphoreType.DMA((3 * CHUNKS + 3,)),
            pltpu.SemaphoreType.DMA((n_head,)),
            pltpu.SemaphoreType.DMA((n_head,)),
            pltpu.SemaphoreType.DMA((16,)),
            pltpu.SemaphoreType.DMA((16,)),
        ],
        compiler_params=pltpu.CompilerParams(
            collective_id=0, has_side_effects=True, vmem_limit_bytes=60 * 2**20
        ),
        name="logsparse_layer",
    )(queries, key_rows, values, out_grad, norm_gain.reshape(1, width), head_levels)
    return normed, dq, dk, dv, gain.reshape(width)


def solution(mesh):
    placed = (
        P("seq", "head"),
        P("seq", "head"),
        P("seq", "head"),
        P("seq", "head"),
        P("head"),
        P("head", None),
    )
    return jax.shard_map(
        body,
        mesh=mesh,
        in_specs=placed,
        out_specs=(
            P("seq", "head"),
            P("seq", "head"),
            P("seq", "head"),
            P("seq", "head"),
            P("head"),
        ),
        check_vma=False,
    )
```

```python
import functools
import math

import jax
import jax.numpy as jnp
from jax import lax
from jax.experimental import pallas as pl
from jax.experimental.pallas import tpu as pltpu
from jax.sharding import PartitionSpec as P

D = 4096
HEAD_DIM = 128
EPSILON = 1e-06
MESH = pl.DeviceIdType.MESH
NEG = -1e30
LOG2E = math.log2(math.e)

VIA8, VIA32 = "via8", "via32"
SLOT = {0: 0, 16: 1, 64: 2, 1: 3, 2: 4, 4: 5, 32: 6, 8: 7, VIA8: 8, VIA32: 9}
BLOCKS = 8
LEVEL = {1: 0, 2: 1, 4: 2, 8: 3, 16: 4, 32: 5, 64: 6}
SEM = {**LEVEL, VIA8: 7, VIA32: 8}
RING = 16
STEP_OWN = (0,)
STEPS_FAR = ((16, 64), (1, 2), (4, 32), (8,))
KEYS, VALUES, QUERIES, GRADS, STATS = range(5)
CHUNKS = 4
FORWARD = tuple((array, chunk) for chunk in range(CHUNKS) for array in (KEYS, VALUES, QUERIES))
BACKWARD = tuple((GRADS, chunk) for chunk in range(CHUNKS))
DIRECT = ((STATS, 0),)
STREAMS = FORWARD + BACKWARD + DIRECT
AROUND8 = ((KEYS, 3), (VALUES, 3), (GRADS, 2), (GRADS, 3))
AROUND32 = ((KEYS, 2), (VALUES, 2), (KEYS, 3), (VALUES, 3), (GRADS, 2), (GRADS, 3))
SEMS = {stream: i for i, stream in enumerate(STREAMS)}


def dot_nt(a, b):
    return lax.dot_general(a, b, (((1,), (1,)), ((), ())), preferred_element_type=jnp.float32)


def dot_nn(a, b):
    return jnp.dot(a, b, preferred_element_type=jnp.float32)


def wide(x, times):
    return x if times == 1 else jnp.concatenate([x] * times, axis=1)


def kernel(
    n_seq,
    n_head,
    heads,
    q_in,
    k_in,
    v_in,
    g_in,
    gain_in,
    levels_in,
    normed_ref,
    dq_ref,
    dk_ref,
    dv_ref,
    gain_out,
    kb,
    vb,
    qb,
    gb,
    tb,
    og,
    gain_ref,
    levels_ref,
    ctx,
    scores,
    acc,
    mx,
    sm,
    dots,
    dk_acc,
    dv_acc,
    ex,
    gain_acc,
    gain_got,
    send_sem,
    recv_sem,
    local_sem,
    ex_send,
    ex_recv,
    gain_send,
    gain_recv,
):
    f32 = jnp.float32
    bf16 = jnp.bfloat16
    rows = q_in.shape[0]
    dim = HEAD_DIM
    scale = 1.0 / math.sqrt(dim)
    scale2 = scale * LOG2E
    me = lax.axis_index("seq")
    my_head = lax.axis_index("head")
    part = heads * dim // CHUNKS
    bufs = {KEYS: kb, VALUES: vb, QUERIES: qb, GRADS: gb, STATS: tb}

    def col(h):
        return pl.ds(pl.multiple_of(h * dim, dim), dim)

    def place(stream):
        return me if stream[0] in (KEYS, VALUES) else n_seq - 1 - me

    def at(stream, spot):
        return spot if stream[0] in (KEYS, VALUES) else n_seq - 1 - spot

    def block(stream, level):
        array, chunk = stream
        size = 2 * heads if array == STATS else rows
        span = pl.ds(SLOT[level] * size, size)
        if stream in DIRECT:
            return bufs[array].at[span] if array == STATS else bufs[array].at[:, span]
        return bufs[array].at[chunk, span]

    def copy(stream, level, source, target):
        return pltpu.make_async_remote_copy(
            src_ref=block(stream, source),
            dst_ref=block(stream, level),
            send_sem=send_sem.at[SEMS[stream], SEM[level]],
            recv_sem=recv_sem.at[SEMS[stream], SEM[level]],
            device_id={"seq": at(stream, target)},
            device_id_type=MESH,
        )

    def spot(stream):
        p = place(stream)
        y = lax.rem(p // 2, 8)
        return p, y, lax.rem(p // RING, 4), p - lax.rem(p, RING)

    def in_ring(p, by):
        y = lax.rem(p // 2 + by, 8)
        return p - lax.rem(p, RING) + 2 * y + lax.rem(p, 2)

    def edges(stream, level):
        p, y, x, base = spot(stream)
        if stream in DIRECT:
            return ((0, p + level, p + level < n_seq),) if level in LEVEL else ()
        if level == 1:
            even = lax.rem(p, 2) == 0
            return ((0, p + 1, even), (2, p - 1, jnp.logical_and(jnp.logical_not(even), p >= 3)))
        if level == 2:
            last = y == 7
            return (
                (0, p + 2, jnp.logical_not(last)),
                (16, p - 14, jnp.logical_and(last, p >= 16)),
            )
        if level in (VIA8, 8) and stream in AROUND8:
            if level == 8:
                return ((VIA8, in_ring(p, 5), arrives(stream, VIA8)),)
            low = y < 4
            target = in_ring(p, 7)
            return (
                (0, target, low),
                (16, target, jnp.logical_and(jnp.logical_not(low), base >= RING)),
            )
        if level in (VIA32, 32) and stream in AROUND32:
            if level == 32:
                return ((VIA32, jnp.where(x == 3, p - 16, p + 48), arrives(stream, VIA32)),)
            return ((0, jnp.where(x == 0, p + 48, p - 16), p + 32 < n_seq),)
        if level not in LEVEL:
            return ()
        source, step = {16: (0, 16), 64: (0, 64), 4: (2, 2), 8: (4, 4), 32: (16, 16)}[level]
        return ((source, p + step, jnp.logical_and(p >= source, p + step < n_seq)),)

    def arrives(stream, level):
        p, y, x, base = spot(stream)
        if level == VIA8:
            return jnp.logical_or(jnp.logical_or(y <= 2, y == 7), base >= RING)
        if level == VIA32:
            return jnp.where(x == 3, p - 48, p + 16) + 32 < n_seq
        return p >= level

    def send(stream, level, source):
        for origin, target, condition in edges(stream, level):
            if origin == source:
                pl.when(condition)(copy(stream, level, origin, target).start)

    def send_done(stream, level):
        for origin, target, condition in edges(stream, level):
            pl.when(condition)(copy(stream, level, origin, target).wait_send)

    def got(stream, level):
        if edges(stream, level):
            there = in_ring(place(stream), 1)
            pl.when(arrives(stream, level))(copy(stream, level, 0, there).wait_recv)

    def pass_on(stream, level):
        got(stream, level)
        for onward in SEM:
            send(stream, onward, level)

    loads = [
        pltpu.make_async_copy(source, target, local_sem.at[i])
        for i, (source, target) in enumerate(
            (
                *(
                    (source.at[:, pl.ds(i * part, part)], target.at[i, pl.ds(0, rows)])
                    for source, target in ((k_in, kb), (v_in, vb), (q_in, qb))
                    for i in range(CHUNKS)
                ),
                (g_in, og),
                (gain_in, gain_ref),
                (levels_in, levels_ref),
            )
        )
    ]
    for load in loads:
        load.start()

    my_core, my_y, my_x, my_z = lax.rem(me, 2), lax.rem(me // 2, 8), lax.rem(me // RING, 4), me // (4 * RING)
    groups = (
        (8, my_y, lambda i: me - 2 * my_y + 2 * i),
        (4, 2 * my_z + my_core, lambda i: me + 4 * RING * (i // 2 - my_z) + lax.rem(i, 2) - my_core),
        (4, my_x, lambda i: me + RING * (i - my_x)),
    )

    barrier = pltpu.get_barrier_semaphore()
    greeted = 0
    partners = [lax.rem(me + step, n_seq) for step in (1, 2, 4, 8, 16, 32, 48, 64, 80, 112, 124, 126)]
    for size, mine, member in groups:
        partners += [member(lax.rem(mine + i, size)) for i in range(1, size)]
    for partner in partners:
        pl.semaphore_signal(barrier, inc=1, device_id={"seq": partner}, device_id_type=MESH)
        greeted += 1
    for step in range(1, n_head):
        pl.semaphore_signal(
            barrier, inc=1, device_id={"head": lax.rem(my_head + step, n_head)}, device_id_type=MESH
        )
        greeted += 1

    for array in bufs:
        size = 2 * heads if array == STATS else rows
        for level in LEVEL:

            @pl.when(place((array, 0)) < level)
            def _(ref=bufs[array], span=pl.ds(SLOT[level] * size, size)):
                if array == STATS:
                    ref[span, :] = jnp.zeros((size, ref.shape[1]), ref.dtype)
                else:
                    for i in range(CHUNKS):
                        ref[i, span, :] = jnp.zeros((size, part), ref.dtype)

    for load in loads:
        load.wait()
    pl.semaphore_wait(barrier, greeted)

    own_order = (16, 64, 2, VIA8, VIA32, 1)
    for arrays in ((KEYS, VALUES), (QUERIES,)):
        for level in own_order:
            for stream in FORWARD:
                if stream[0] in arrays:
                    send(stream, level, 0)

    def bias_of(h, level, stream):
        if level == 0:
            return jnp.float32(0.0)
        live = jnp.logical_and(levels_ref[h, LEVEL[level]] == 1, place(stream) >= level)
        return jnp.where(live, jnp.float32(0.0), jnp.float32(NEG))

    row_id = lax.broadcasted_iota(jnp.int32, (rows, rows), 0)
    col_id = lax.broadcasted_iota(jnp.int32, (rows, rows), 1)

    per_chunk = heads // CHUNKS

    def each_head(body):
        def some(i, carry):
            for j in range(per_chunk):
                body(i * per_chunk + j, lambda ref, span: ref[i, span, j * dim : (j + 1) * dim])
            return carry

        lax.fori_loop(0, CHUNKS, some, 0)

    def forward_step(step):
        first = step == STEP_OWN
        top = SLOT[step[0]] * rows
        count = len(step) * rows

        def one(h, of):
            q = of(qb, slice(0, rows))
            k = of(kb, slice(top, top + count))
            v = of(vb, slice(top, top + count))
            s = dot_nt(q, k) * scale2
            if first:
                s = jnp.where(col_id <= row_id, s, NEG)
                high = s
            else:
                parts = [
                    s[:, j * rows : (j + 1) * rows] + bias_of(h, level, (KEYS, 0))
                    for j, level in enumerate(step)
                ]
                high = functools.reduce(jnp.maximum, parts)
                s = parts[0] if len(parts) == 1 else jnp.concatenate(parts, axis=1)
            scores[h, :, top : top + count] = s
            new = jnp.broadcast_to(jnp.max(high, axis=1, keepdims=True), (rows, dim))
            if not first:
                old = mx[h]
                new = jnp.maximum(old, new)
            p = jnp.exp2(s - wide(new, len(step)))
            total = functools.reduce(
                jnp.add, [p[:, j * rows : (j + 1) * rows] for j in range(len(step))]
            )
            total = jnp.broadcast_to(jnp.sum(total, axis=1, keepdims=True), (rows, dim))
            out = dot_nn(p.astype(bf16), v)
            if first:
                acc[:, col(h)] = out
                sm[h] = total
            else:
                fade = jnp.exp2(old - new)
                acc[:, col(h)] = acc[:, col(h)] * fade + out
                sm[h] = sm[h] * fade + total
            mx[h] = new

        each_head(one)

    def forward_got(level):
        for stream in FORWARD:
            if stream[0] != QUERIES:
                got(stream, level)

    forward_step(STEP_OWN)
    ordered = sorted(FORWARD, key=lambda stream: stream[0] == QUERIES)
    for stream in ordered:
        if stream[0] != QUERIES:
            for level in (16, 2, VIA8, VIA32):
                pass_on(stream, level)
    for stream in ordered:
        if stream[0] == QUERIES:
            pass_on(stream, 16)
            pass_on(stream, 2)
        else:
            pass_on(stream, 4)
    forward_got(64)
    forward_step((16, 64))
    for stream in ordered:
        if stream[0] == QUERIES:
            pass_on(stream, 4)
    forward_got(1)
    forward_step((1, 2))
    forward_got(32)
    forward_step((4, 32))
    forward_got(8)
    forward_step((8,))

    def finish(h, carry):
        squares, pulls = carry
        total = sm[h]
        c = (acc[:, col(h)] * (1.0 / total)).astype(bf16)
        ctx[:, col(h)] = c
        c = c.astype(f32)
        lse = mx[h] + jnp.log2(total)
        mx[h] = lse
        tb[pl.ds(h, 1), :] = lse.T[0:1, :]
        pull = gain_ref[0:1, col(h)] * og[:, col(h)].astype(f32) * c
        return squares + c * c, pulls + pull

    zero = jnp.zeros((rows, dim), f32)
    squares, pulls = lax.fori_loop(0, heads, finish, (zero, zero))
    ex[0, 0:1, :] = jnp.sum(squares.T, axis=0, keepdims=True)
    ex[0, 1:2, :] = jnp.sum(pulls.T, axis=0, keepdims=True)
    ex[0, 2:8, :] = jnp.zeros((6, rows), f32)
    swaps = [
        pltpu.make_async_remote_copy(
            src_ref=ex.at[0],
            dst_ref=ex.at[step],
            send_sem=ex_send.at[step],
            recv_sem=ex_recv.at[step],
            device_id={"head": lax.rem(my_head + step, n_head)},
            device_id_type=MESH,
        )
        for step in range(1, n_head)
    ]
    for one in swaps:
        one.start()
    for one in swaps:
        one.wait()
    whole = functools.reduce(jnp.add, [ex[step] for step in range(n_head)])
    inverse_row = lax.rsqrt(whole[0:1, :] / D + EPSILON)
    pull_row = inverse_row * inverse_row * inverse_row * whole[1:2, :] / D
    inverse = jnp.broadcast_to(inverse_row, (dim, rows)).T
    pull_back = jnp.broadcast_to(pull_row, (dim, rows)).T

    def make_grad(chunk, j):
        h = chunk * per_chunk + j
        c = ctx[:, col(h)].astype(f32)
        scaled = gain_ref[0:1, col(h)] * og[:, col(h)].astype(f32)
        gb[chunk, 0:rows, j * dim : (j + 1) * dim] = (inverse * scaled - pull_back * c).astype(bf16)

    for stream in BACKWARD:
        for i in range(per_chunk):
            make_grad(stream[1], i)
        for level in own_order:
            send(stream, level, 0)

    def make_dots(h, of):
        c = ctx[:, col(h)].astype(f32)
        both = of(gb, slice(0, rows)).astype(f32) * c
        row = jnp.sum(both.T, axis=0, keepdims=True)
        tb[pl.ds(heads + h, 1), :] = row
        dots[h] = jnp.broadcast_to(row, (dim, rows)).T

    each_head(make_dots)
    for level in (8, 4, 2, 1, 32, 16, 64):
        send((STATS, 0), level, 0)

    def make_normed(h, of):
        c = ctx[:, col(h)].astype(f32) * inverse
        normed_ref[:, col(h)] = (c * gain_ref[0:1, col(h)]).astype(bf16)
        gain_acc[0:1, col(h)] = jnp.sum(og[:, col(h)].astype(f32) * c, axis=0, keepdims=True)

    def gain_copies(r):
        size, mine, member = groups[r]
        first = sum(group[0] for group in groups[:r])
        return first, [
            pltpu.make_async_remote_copy(
                src_ref=gain_acc,
                dst_ref=gain_got.at[first + mine],
                send_sem=gain_send.at[first + i],
                recv_sem=gain_recv.at[first + i],
                device_id={"seq": member(lax.rem(mine + i, size))},
                device_id_type=MESH,
            )
            for i in range(1, size)
        ]

    def gain_start(r):
        first, copies = gain_copies(r)
        for one in copies:
            one.start()
        gain_got[first + groups[r][1]] = gain_acc[...]

    def gain_end(r):
        first, copies = gain_copies(r)
        for one in copies:
            one.wait()
        gain_acc[...] = functools.reduce(
            jnp.add, [gain_got[first + i] for i in range(groups[r][0])]
        )

    def query_side(h, of):
        g = of(gb, slice(0, rows))
        lse = mx[h]
        dot = dots[h]
        total = jnp.zeros((rows, dim), f32)
        for j in range(0, BLOCKS, 2):
            span = slice(j * rows, (j + 2) * rows)
            pull = dot_nt(g, of(vb, span))
            p = jnp.exp2(scores[h, :, span] - wide(lse, 2))
            ds = (p * (pull - wide(dot, 2))).astype(bf16)
            total = total + dot_nn(ds, of(kb, span))
        dq_ref[:, col(h)] = (total * scale).astype(bf16)

    def key_step(step):
        first = step == STEP_OWN
        slot = SLOT[step[0]]
        top = slot * rows
        count = len(step) * rows

        def one(h, of):
            k = of(kb, slice(0, rows))
            v = of(vb, slice(0, rows))
            q = of(qb, slice(top, top + count))
            g = of(gb, slice(top, top + count))
            shift = []
            dot = []
            for j, level in enumerate(step):
                base = (slot + j) * 2 * heads
                shift.append(bias_of(h, level, (QUERIES, 0)) - tb[pl.ds(base + h, 1), :])
                dot.append(tb[pl.ds(base + heads + h, 1), :])
            shift = wide(shift[0], 1) if len(step) == 1 else jnp.concatenate(shift, axis=1)
            dot = wide(dot[0], 1) if len(step) == 1 else jnp.concatenate(dot, axis=1)
            s = dot_nt(k, q) * scale2 + shift
            if first:
                s = jnp.where(row_id <= col_id, s, NEG)
            p = jnp.exp2(s)
            pull = dot_nt(v, g)
            ds = (p * (pull - dot)).astype(bf16)
            dv = dot_nn(p.astype(bf16), g)
            dk = dot_nn(ds, q)
            if first:
                dv_acc[:, col(h)] = dv
                dk_acc[:, col(h)] = dk
            elif step == STEPS_FAR[-1]:
                dv_ref[:, col(h)] = (dv_acc[:, col(h)] + dv).astype(bf16)
                dk_ref[:, col(h)] = ((dk_acc[:, col(h)] + dk) * scale).astype(bf16)
            else:
                dv_acc[:, col(h)] += dv
                dk_acc[:, col(h)] += dk

        each_head(one)

    def key_got(level):
        for stream in BACKWARD + DIRECT:
            got(stream, level)
        for stream in FORWARD:
            if stream[0] == QUERIES:
                got(stream, level)

    each_head(make_normed)
    gain_start(0)
    for stream in BACKWARD:
        for level in (16, 2, VIA8, VIA32):
            pass_on(stream, level)
    key_step(STEP_OWN)
    gain_end(0)
    gain_start(1)
    for stream in BACKWARD:
        pass_on(stream, 4)
    each_head(query_side)
    gain_end(1)
    gain_start(2)
    for stream in DIRECT:
        for level in (16, 2, 4):
            got(stream, level)
    key_got(64)
    key_step((16, 64))
    key_got(1)
    key_step((1, 2))
    gain_end(2)
    gain_out[...] = gain_acc[...] * (1.0 / math.sqrt(n_seq * rows))
    key_got(32)
    key_step((4, 32))
    key_got(8)
    key_step((8,))

    for stream in STREAMS:
        for level in SEM:
            send_done(stream, level)


def hand_over(*refs):
    for source, target in zip(refs[:5], refs[5:]):
        target[...] = source[...]


def body(queries, key_rows, values, out_grad, norm_gain, head_levels):
    f32 = jnp.float32
    bf16 = jnp.bfloat16
    rows, width = queries.shape
    heads = width // HEAD_DIM
    n_seq = lax.axis_size("seq")
    n_head = lax.axis_size("head")
    slots = BLOCKS
    stops = len(SLOT)
    full = jax.ShapeDtypeStruct((rows, width), bf16)
    hbm = pl.BlockSpec(memory_space=pltpu.HBM)
    vmem = pl.BlockSpec(memory_space=pltpu.VMEM)
    results = pl.pallas_call(
        functools.partial(kernel, n_seq, n_head, heads),
        out_shape=(full, full, full, full, jax.ShapeDtypeStruct((1, width), f32)),
        in_specs=[hbm] * 6,
        out_specs=[vmem] * 5,
        scratch_shapes=[
            pltpu.VMEM((CHUNKS, stops * rows, width // CHUNKS), bf16),
            pltpu.VMEM((CHUNKS, stops * rows, width // CHUNKS), bf16),
            pltpu.VMEM((CHUNKS, slots * rows, width // CHUNKS), bf16),
            pltpu.VMEM((CHUNKS, stops * rows, width // CHUNKS), bf16),
            pltpu.VMEM((slots * 2 * heads, rows), f32),
            pltpu.VMEM((rows, width), bf16),
            pltpu.VMEM((1, width), f32),
            pltpu.SMEM(head_levels.shape, jnp.int32),
            pltpu.VMEM((rows, width), bf16),
            pltpu.VMEM((heads, rows, slots * rows), f32),
            pltpu.VMEM((rows, width), f32),
            pltpu.VMEM((heads, rows, HEAD_DIM), f32),
            pltpu.VMEM((heads, rows, HEAD_DIM), f32),
            pltpu.VMEM((heads, rows, HEAD_DIM), f32),
            pltpu.VMEM((rows, width), f32),
            pltpu.VMEM((rows, width), f32),
            pltpu.VMEM((n_head, 8, rows), f32),
            pltpu.VMEM((1, width), f32),
            pltpu.VMEM((16, 1, width), f32),
            pltpu.SemaphoreType.DMA((len(STREAMS), len(SEM))),
            pltpu.SemaphoreType.DMA((len(STREAMS), len(SEM))),
            pltpu.SemaphoreType.DMA((3 * CHUNKS + 3,)),
            pltpu.SemaphoreType.DMA((n_head,)),
            pltpu.SemaphoreType.DMA((n_head,)),
            pltpu.SemaphoreType.DMA((16,)),
            pltpu.SemaphoreType.DMA((16,)),
        ],
        compiler_params=pltpu.CompilerParams(
            collective_id=0, has_side_effects=True, vmem_limit_bytes=60 * 2**20
        ),
        name="logsparse_layer",
    )(queries, key_rows, values, out_grad, norm_gain.reshape(1, width), head_levels)
    normed, dq, dk, dv, gain = pl.pallas_call(
        hand_over,
        out_shape=(full, full, full, full, jax.ShapeDtypeStruct((1, width), f32)),
        in_specs=[vmem] * 5,
        out_specs=[vmem] * 5,
        name="hand_over",
    )(*results)
    return normed, dq, dk, dv, gain.reshape(width)


def solution(mesh):
    placed = (
        P("seq", "head"),
        P("seq", "head"),
        P("seq", "head"),
        P("seq", "head"),
        P("head"),
        P("head", None),
    )
    return jax.shard_map(
        body,
        mesh=mesh,
        in_specs=placed,
        out_specs=(
            P("seq", "head"),
            P("seq", "head"),
            P("seq", "head"),
            P("seq", "head"),
            P("head"),
        ),
        check_vma=False,
    )
```
